256 devices in a mesh: row: 8 (over y, core), col: 32 (over z, x).
Axes of the slice: x: 4, y: 4, z: 8, core: 2. Of those that a mesh axis runs over, the one named last changes fastest.
Arguments:
- images: float32 [16384, 1152], P(('row', 'col')), may hold values from -170 to 170
- texts: float32 [16384, 1152], P(('col', 'row')), may hold values from -170 to 170
- logit_scale: float32 [1], replicated, may hold values from 4 to 16
- logit_bias: float32 [1], replicated, may hold values from -6 to -1
Outputs:
- image_step: float32 [16384, 1152], P(('row', 'col'))
- text_step: float32 [16384, 1152], P(('col', 'row'))
- loss: float32 [1], replicated
The draws below stay inside these ranges and needn't reach their ends.
All inputs are finite; a program needn't handle non-finite values.
Results may differ from the reference program's by a relative error of at most 0.0003.
Values sent between devices are 32-bit elements; how exact they have to be, the bound alone decides.
No kernel may reach another device: no remote copies, remote signals or barrier semaphores. Data moves between devices by JAX's collectives and lax.ppermute only.
A program may use at most 64 MiB of HBM per device.

```python
import math
import jax
import jax.numpy as jnp
from jax import lax

D = 1152
N = 16384


def shared_base(key):
    first = jax.random.truncated_normal(jax.random.fold_in(key, 11), -6.0, 6.0, (N, D), jnp.float32)
    return first


def scale_table(key, spread):
    places = jnp.arange(N, dtype=jnp.float32) / N
    lift = jax.random.uniform(jax.random.fold_in(key, 21), (N, 1), jnp.float32)
    row_scale = jnp.exp(jnp.log(spread) * lift) * jnp.exp(-jnp.log(3.0) * places)[:, None]
    col_scale = jax.random.uniform(jax.random.fold_in(key, 22), (1, D), jnp.float32, 1.0, 2.0)
    return row_scale * col_scale


def draw_images(key, part):
    spread = 10.0
    base = shared_base(key)
    key = jax.random.fold_in(key, 3)
    return base * scale_table(key, spread)


def draw_texts(key, part):
    spread = 10.0
    base = shared_base(key)
    key = jax.random.fold_in(key, 4)
    noise = jax.random.truncated_normal(jax.random.fold_in(key, 31), -6.0, 6.0, (N, D), jnp.float32)
    return (0.8 * base + 0.6 * noise) * scale_table(key, spread)


def setup_inputs(seed: int = 0) -> dict:
    splits = jax.random.split(jax.random.key(seed), 5)
    return {
        "images": draw_images(jax.random.fold_in(splits[4], 71), 0),
        "texts": draw_texts(jax.random.fold_in(splits[4], 71), 0),
        "logit_scale": jnp.clip(jax.random.uniform(splits[2], (1,), jnp.float32, 4.0, 16.0), 4.0, 16.0),
        "logit_bias": jnp.clip(jax.random.uniform(splits[3], (1,), jnp.float32, -6.0, -1.0), -6.0, -1.0),
    }


EPS = 1e-06
HIGH = lax.Precision.HIGHEST

def unit_rows(values):
    length = jnp.sqrt(lax.optimization_barrier(jnp.sum(values * values, axis=1, keepdims=True)) + EPS)
    return (values / length, length)

def back_rows(grad_unit, unit, length):
    inner = lax.optimization_barrier(jnp.sum(unit * grad_unit, axis=1, keepdims=True))
    return (grad_unit - unit * inner) / length

def reference(images, texts, logit_scale, logit_bias):
    total = images.shape[0]
    width = images.shape[1]
    image_unit, image_len = unit_rows(images)
    text_unit, text_len = unit_rows(texts)
    scale = logit_scale[0]
    shift = logit_bias[0]
    block = math.gcd(512, total)
    text_ids = jnp.arange(total, dtype=jnp.int32)

    def step(text_sum, index):
        start = (index * block).astype(jnp.int32)
        piece = lax.dynamic_slice_in_dim(image_unit, start, block, 0)
        ids = start + jnp.arange(block, dtype=jnp.int32)
        cosine = jnp.dot(piece, text_unit.T, precision=HIGH, preferred_element_type=jnp.float32)
        logits = scale * cosine + shift
        match = ids[:, None] == text_ids[None, :]
        part_loss = jnp.sum(jnp.where(match, jax.nn.softplus(-logits), jax.nn.softplus(logits)))
        weight = jnp.where(match, -jax.nn.sigmoid(-logits), jax.nn.sigmoid(logits))
        image_part = scale * jnp.dot(weight, text_unit, precision=HIGH, preferred_element_type=jnp.float32)
        text_sum = text_sum + scale * jnp.dot(weight.T, piece, precision=HIGH, preferred_element_type=jnp.float32)
        return (text_sum, (image_part, part_loss))
    start_sum = jnp.zeros((total, width), jnp.float32)
    text_grad_unit, (image_parts, losses) = lax.scan(step, start_sum, jnp.arange(total // block, dtype=jnp.int32))
    image_grad_unit = image_parts.reshape(total, width)
    image_grad = back_rows(image_grad_unit, image_unit, image_len)
    text_grad = back_rows(text_grad_unit, text_unit, text_len)
    squares = jnp.sum(image_grad * image_grad) + jnp.sum(text_grad * text_grad)
    factor = lax.rsqrt(squares / (2.0 * total * width) + EPS)
    loss = (jnp.sum(losses) / (1.0 * total * total)).reshape(1)
    return (image_grad * factor, text_grad * factor, loss)
```

```python
import functools

import jax
import jax.numpy as jnp
from jax import lax
from jax.experimental import pallas as pl
from jax.experimental.pallas import tpu as pltpu
from jax.sharding import Mesh, PartitionSpec as P

EPS = 1e-06
F32 = jnp.float32
BF16 = jnp.bfloat16
SIZES = {"y": 4, "core": 2, "z": 8, "x": 4}
NAMES = tuple(SIZES)
DEVICES = 256
VMEM = pl.BlockSpec(memory_space=pltpu.VMEM)
SMEM = pl.BlockSpec(memory_space=pltpu.SMEM)
LIMIT = 58 * 1024 * 1024


def call(body, out_shape, args, specs=None, out_specs=None, scratch=(), flops=0, nbytes=0):
    return pl.pallas_call(
        body,
        out_shape=out_shape,
        in_specs=specs or [VMEM] * len(args),
        out_specs=out_specs or jax.tree.map(lambda _: VMEM, out_shape),
        scratch_shapes=list(scratch),
        compiler_params=pltpu.CompilerParams(vmem_limit_bytes=LIMIT),
        cost_estimate=pl.CostEstimate(flops=flops, bytes_accessed=nbytes, transcendentals=0),
    )(*args)


def sds(shape, dtype=F32):
    return jax.ShapeDtypeStruct(shape, dtype)


def shift(value, axis, step):
    n = SIZES[axis]
    return lax.ppermute(value, axis, [(i, (i + step) % n) for i in range(n)])


def unit_body(image, text, image_unit, image_len, text_unit, text_len):
    for src, unit, length in ((text, text_unit, text_len), (image, image_unit, image_len)):
        v = src[...]
        n = jnp.sqrt(jnp.sum(v * v, axis=1, keepdims=True) + EPS)
        unit[...] = v / n
        length[...] = jnp.broadcast_to(n, length.shape)


def gather_half(value, first, second):
    h = value.shape[0]
    near = jnp.concatenate([value] + [shift(value, first, k) for k in (1, 2, 3)], axis=0)
    up = shift(near, second, 1)
    down = shift(near, second, -1)
    return [near, up, down, shift(up[: 2 * h], second, 1), shift(down[2 * h :], second, -1)]


def half_places(first, second):
    near = [0, -1, -2, -3]
    return [(f, s) for s in (0, -1, 1) for f in near] + [(f, 2) for f in near]


def reduce_half(parts, first, second):
    near, up, down, far_up, far_down = parts
    h = near.shape[0] // 4
    head = up[: 2 * h] + shift(far_up, second, -1)
    tail = down[2 * h :] + shift(far_down, second, 1)
    up = jnp.concatenate([head, up[2 * h :]], axis=0)
    down = jnp.concatenate([down[: 2 * h], tail], axis=0)
    near = near + shift(up, second, -1) + shift(down, second, 1)
    return [near[:h]] + [shift(near[k * h : (k + 1) * h], first, -k) for k in (1, 2, 3)]


def split(v):
    hi = v.astype(BF16)
    return hi, (v - hi.astype(F32)).astype(BF16)


def fold(v):
    r, c = v.shape
    v = v.reshape(r // 8, 8, c).sum(axis=0)
    out = v[:, :128]
    for k in range(1, c // 128):
        out = out + v[:, k * 128 : (k + 1) * 128]
    return out


def weight_body(counts, chunk, *refs):
    n = len(counts)
    pieces = refs[:n]
    text, image_id, text_id, scal, core = refs[n : n + 5]
    ih, il, th, tl, wh, wl, loss, i3, t3 = refs[n + 5 :]
    d = ih.shape[1]
    m, rows = text.shape[0], text.shape[2]
    mine = core[0]

    @pl.loop(0, m)
    def _(z):
        for side, c in ((0, mine), (1, 1 - mine)):
            hi, lo = split(text[z, c])
            at = pl.ds(pl.multiple_of((side * m + z) * rows, rows), rows)
            th[at, :] = hi
            tl[at, :] = lo
            t3[at, :d] = hi
            t3[at, d : 2 * d] = hi
            t3[at, 2 * d :] = lo

    start = 0
    for piece, count in zip(pieces, counts):
        hi, lo = split(piece[...])
        at = slice(start, start + count)
        ih[at, :] = hi
        il[at, :] = lo
        i3[at, :d] = hi
        i3[at, d : 2 * d] = lo
        i3[at, 2 * d :] = hi
        start += count
    scale, bias = scal[0], scal[1]
    total = jnp.zeros((8, 128), F32)
    for k in range(start // chunk):
        at = slice(k * chunk, (k + 1) * chunk)
        cosine = lax.dot_general(
            i3[at, :], t3[...], (((1,), (1,)), ((), ())), preferred_element_type=F32
        )
        logits = scale * cosine + bias
        sign = jnp.where(image_id[at, :] == text_id[...], -1.0, 1.0)
        x = sign * logits
        e = jnp.exp(-jnp.abs(x))
        u = 1.0 + e
        r = 1.0 / u
        total = total + fold(jnp.maximum(x, 0.0) + jnp.log(u) + (e - (u - 1.0)) * r)
        w = sign * jnp.where(x >= 0.0, r, e * r)
        hi, lo = split(w)
        wh[at, :] = hi
        wl[at, :] = lo
    loss[...] = total


def product(a_hi, a_lo, b_hi, b_lo, dims):
    dot = functools.partial(
        lax.dot_general, dimension_numbers=(dims, ((), ())), preferred_element_type=F32
    )
    return dot(a_hi, b_hi) + (dot(a_lo, b_hi) + dot(a_hi, b_lo))


def text_body(chunk, wh, wl, ih, il, mine, other):
    m = mine.shape[0]
    for out, base in ((other, m), (mine, 0)):
        for k in range(m // chunk):
            at = slice(base + k * chunk, base + (k + 1) * chunk)
            out[k * chunk : (k + 1) * chunk, :] = product(
                wh[:, at], wl[:, at], ih[...], il[...], ((0,), (0,))
            )


def image_body(counts, wh, wl, th, tl, *outs):
    start = 0
    for out, count in zip(outs, counts):
        at = slice(start, start + count)
        out[...] = product(wh[at, :], wl[at, :], th[...], tl[...], ((1,), (0,)))
        start += count


def back_body(*refs):
    a = refs[0:4]
    b = refs[4:8]
    text_sum, image_unit, image_len, text_unit, text_len, loss, scal = refs[8:15]
    image_grad, text_grad, send = refs[15:]
    scale = scal[0]
    h = a[0].shape[0]
    squares = jnp.zeros((1, 1), F32)
    jobs = (
        (image_grad, image_unit, image_len, 0, h, lambda: a[0][...] + a[1][...] + a[2][...] + a[3][...]),
        (image_grad, image_unit, image_len, h, h, lambda: b[0][...] + b[1][...] + b[2][...] + b[3][...]),
        (text_grad, text_unit, text_len, 0, 2 * h, lambda: text_sum[...]),
    )
    for out, unit, length, start, count, load in jobs:
        at = slice(start, start + count)
        g = scale * load()
        u = unit[at, :]
        inner = jnp.sum(u * g, axis=1, keepdims=True)
        v = (g - u * inner) / length[at, :1]
        out[at, :] = v
        s = jnp.sum(v * v, axis=1, keepdims=True)
        squares = squares + jnp.sum(s, axis=0, keepdims=True)
    s = jnp.sum(loss[...], axis=1, keepdims=True)
    loss_sum = jnp.sum(s, axis=0, keepdims=True)
    lane = lax.broadcasted_iota(jnp.int32, send.shape, 2)
    send[...] = jnp.where(lane == 0, squares[None], jnp.where(lane == 1, loss_sum[None], 0.0))


def step_body(total, width, image_grad, text_grad, got, image_step, text_step, loss):
    sums = jnp.sum(got[...], axis=0)
    factor = lax.rsqrt(sums[:, 0:1] / (2.0 * total * width) + EPS)
    image_step[...] = image_grad[...] * factor
    text_step[...] = text_grad[...] * factor
    loss[0] = sums[0, 1] / (1.0 * total * total)


def local(images, texts, logit_scale, logit_bias):
    rows, d = images.shape
    h = rows // 2
    n = DEVICES * rows
    tile = 16 * rows
    y, core, z, x = (lax.axis_index(a).astype(jnp.int32) for a in NAMES)
    scal = jnp.concatenate([logit_scale, logit_bias])
    unit, lens = sds((rows, d)), sds((rows, 128))
    image_unit, image_len, text_unit, text_len = call(
        unit_body, (unit, lens, unit, lens), (images, texts), nbytes=4 * rows * d * 4
    )
    text_tile = lax.all_gather(text_unit, ("z", "core"), axis=0, tiled=False)
    text_tile = text_tile.reshape(SIZES["z"], 2, rows, d)
    pieces_a = gather_half(image_unit[:h], "x", "y")
    pieces_b = gather_half(image_unit[h:], "y", "x")
    pieces = pieces_a + pieces_b
    counts = tuple(p.shape[0] for p in pieces)

    spot = jnp.arange(h, dtype=jnp.int32)
    ids = []
    for half, names in ((0, ("x", "y")), (1, ("y", "x"))):
        for first, second in half_places(*names):
            off = dict(zip(names, (first, second)))
            iy, ix = (y + off["y"]) % 4, (x + off["x"]) % 4
            ids.append((((iy * 2 + core) * 8 + z) * 4 + ix) * rows + half * h + spot)
    image_id = jnp.concatenate(ids).reshape(tile, 1)
    z_all = jnp.arange(SIZES["z"], dtype=jnp.int32)[None, :, None]
    c_all = jnp.stack([core, 1 - core])[:, None, None]
    row_all = jnp.arange(rows, dtype=jnp.int32)[None, None, :]
    text_id = ((((z_all * 4 + x) * 4 + y) * 2 + c_all) * rows + row_all).reshape(1, tile)

    half_in = sds((tile, d), BF16)
    half_w = sds((tile, tile), BF16)
    work = 6 * tile * tile * d
    chunk = min(256, tile)
    ih, il, th, tl, wh, wl, loss = call(
        functools.partial(weight_body, counts, chunk),
        (half_in, half_in, half_in, half_in, half_w, half_w, sds((8, 128))),
        (*pieces, text_tile, image_id, text_id, scal, core.reshape(1)),
        specs=[VMEM] * (len(pieces) + 3) + [SMEM, SMEM],
        scratch=[pltpu.VMEM((tile, 3 * d), BF16)] * 2,
        flops=work,
        nbytes=tile * d * 16,
    )
    side = sds((tile // 2, d))
    mine, other = call(
        functools.partial(text_body, min(256, tile // 2)),
        (side, side),
        (wh, wl, ih, il),
        flops=work,
        nbytes=tile * d * 12,
    )
    mine = mine + shift(other, "core", 1)
    text_sum = lax.psum_scatter(mine, "z", scatter_dimension=0, tiled=True)
    parts = call(
        functools.partial(image_body, counts),
        tuple(sds((c, d)) for c in counts),
        (wh, wl, th, tl),
        flops=work,
        nbytes=tile * d * 12,
    )
    sums_a = reduce_half(parts[:5], "x", "y")
    sums_b = reduce_half(parts[5:], "y", "x")
    row = sds((rows, d))
    image_grad, text_grad, send = call(
        back_body,
        (row, row, sds((DEVICES, 1, 128))),
        (*sums_a, *sums_b, text_sum, image_unit, image_len, text_unit, text_len, loss, scal),
        specs=[VMEM] * 14 + [SMEM],
    )
    got = lax.all_to_all(send, NAMES, 0, 0)
    image_step, text_step, loss = call(
        functools.partial(step_body, n, d),
        (row, row, sds((1,))),
        (image_grad, text_grad, got),
        out_specs=(VMEM, VMEM, SMEM),
    )
    return image_step, text_step, loss


def solution(mesh):
    fine = Mesh(mesh.devices.reshape(tuple(SIZES.values())), NAMES)
    image_spec = P(("y", "core", "z", "x"), None)
    text_spec = P(("z", "x", "y", "core"), None)
    return jax.shard_map(
        local,
        mesh=fine,
        in_specs=(image_spec, text_spec, P(), P()),
        out_specs=(image_spec, text_spec, P()),
        check_vma=False,
    )
```

```python
import functools

import jax
import jax.numpy as jnp
from jax import lax
from jax.experimental import pallas as pl
from jax.experimental.pallas import tpu as pltpu
from jax.sharding import Mesh, PartitionSpec as P

EPS = 1e-06
F32 = jnp.float32
BF16 = jnp.bfloat16
F8 = jnp.float8_e4m3fn
HIGH_UP = 2.0**8
LOW_UP = 2.0**17
SIZES = {"y": 4, "core": 2, "z": 8, "x": 4}
NAMES = tuple(SIZES)
DEVICES = 256
VMEM = pl.BlockSpec(memory_space=pltpu.VMEM)
SMEM = pl.BlockSpec(memory_space=pltpu.SMEM)


def call(body, out_shape, args, specs=None, out_specs=None, scratch=(), limit=8, flops=0, nbytes=0):
    return pl.pallas_call(
        body,
        out_shape=out_shape,
        in_specs=specs or [VMEM] * len(args),
        out_specs=out_specs or jax.tree.map(lambda _: VMEM, out_shape),
        scratch_shapes=list(scratch),
        compiler_params=pltpu.CompilerParams(vmem_limit_bytes=limit * 1024 * 1024),
        cost_estimate=pl.CostEstimate(flops=flops, bytes_accessed=nbytes, transcendentals=0),
    )(*args)


def sds(shape, dtype=F32):
    return jax.ShapeDtypeStruct(shape, dtype)


def shift(value, axis, step):
    n = SIZES[axis]
    return lax.ppermute(value, axis, [(i, (i + step) % n) for i in range(n)])


def unit_rows(v):
    length = jnp.sqrt(jnp.sum(v * v, axis=1, keepdims=True) + EPS)
    return v / length, length


def unit_body(image, first, second):
    h = first.shape[0]
    first[...] = unit_rows(image[:h, :])[0]
    second[...] = unit_rows(image[h:, :])[0]


def gather_half(value, first, second):
    h = value.shape[0]
    near = jnp.concatenate([value] + [shift(value, first, k) for k in (1, 2, 3)], axis=0)
    up = shift(near, second, 1)
    down = shift(near, second, -1)
    return [near, up, down, shift(up[: 2 * h], second, 1), shift(down[2 * h :], second, -1)]


def half_places():
    near = [0, -1, -2, -3]
    return [(f, s) for s in (0, -1, 1) for f in near] + [(f, 2) for f in near]


def reduce_half(parts, first, second):
    near, up, down, far_up, far_down = parts
    h = near.shape[0] // 4
    head = up[: 2 * h] + shift(far_up, second, -1)
    tail = down[2 * h :] + shift(far_down, second, 1)
    up = jnp.concatenate([head, up[2 * h :]], axis=0)
    down = jnp.concatenate([down[: 2 * h], tail], axis=0)
    near = near + shift(up, second, -1) + shift(down, second, 1)
    return [near[:h]] + [shift(near[k * h : (k + 1) * h], first, -k) for k in (1, 2, 3)]


def split(v):
    hi = v.astype(BF16)
    return hi, v - hi.astype(F32)


def small(hi, lo):
    return (hi.astype(F32) * HIGH_UP).astype(F8), (lo * LOW_UP).astype(F8)


def fold(v):
    r, c = v.shape
    v = v.reshape(r // 8, 8, c).sum(axis=0)
    out = v[:, :128]
    for k in range(1, c // 128):
        out = out + v[:, k * 128 : (k + 1) * 128]
    return out


def weight_body(places, chunk, counts, kept, *refs):
    n = len(counts)
    pieces = refs[:n]
    text, scal, spot = refs[n : n + 3]
    outs, loss = refs[n + 3 : n + 3 + len(kept)], refs[n + 3 + len(kept)]
    ih, ih8, il8, th, th8, tl8, wh, wh8, wl8, image_in, text_in, result, in_sems, sems = refs[
        n + 4 + len(kept) :
    ]
    m, rows = text.shape[0], text.shape[2]
    tile = ih.shape[0]
    h = rows // 2
    y, core, z, x = (spot[k] for k in range(4))

    image_copies, start = [], 0
    for k, count in enumerate(counts):
        at = pl.ds(start, count)
        image_copies.append(pltpu.make_async_copy(pieces[k], image_in.at[at], in_sems.at[k]))
        start += count
    text_copies = [
        pltpu.make_async_copy(text.at[k], text_in.at[k], in_sems.at[n + k]) for k in range(m)
    ]
    for copy in image_copies + text_copies:
        copy.start()

    start = 0
    for copy, count in zip(image_copies, counts):
        copy.wait()
        at = slice(start, start + count)
        hi, lo = split(image_in[at, :])
        ih[at, :] = hi
        ih8[at, :], il8[at, :] = small(hi, lo)
        start += count
    for k, copy in enumerate(text_copies):
        copy.wait()
        for c in (0, 1):
            at = slice((c * m + k) * rows, (c * m + k + 1) * rows)
            v = text_in[k, core if c == 0 else 1 - core]
            length = jnp.sqrt(jnp.sum(v * v, axis=1, keepdims=True) + EPS)
            hi, lo = split(v * (1.0 / length))
            th[at, :] = hi
            th8[at, :], tl8[at, :] = small(hi, lo)

    col = lax.broadcasted_iota(jnp.int32, (1, tile), 1)
    block = col // rows
    side = block // m
    text_core = jnp.where(side == 0, core, 1 - core)
    text_id = ((((block - side * m) * 4 + x) * 4 + y) * 2 + text_core) * rows + col % rows
    scale, bias = scal[0], scal[1]
    texts_in = (th[...], th8[...], tl8[...])

    def finish(at, cosine):
        logits = scale * cosine + bias
        parts = []
        for half, dy, dx in places[at.start // h : at.stop // h]:
            iy, ix = (y + dy) % 4, (x + dx) % 4
            first = (((iy * 2 + core) * 8 + z) * 4 + ix) * rows + half * h
            parts.append(first + lax.broadcasted_iota(jnp.int32, (h, 1), 0))
        image_id = jnp.concatenate(parts, axis=0)
        sign = jnp.where(image_id == text_id, -1.0, 1.0)
        v = sign * logits
        e = jnp.exp(-jnp.abs(v))
        u = 1.0 + e
        r = 1.0 / u
        w = sign * jnp.where(v >= 0.0, r, e * r)
        hi, lo = split(w)
        wh[at, :] = hi
        wh8[at, :], wl8[at, :] = small(hi, lo)
        return fold(jnp.maximum(v, 0.0) + jnp.log(u) + (e - (u - 1.0)) * r)

    total = jnp.zeros((8, 128), F32)
    for low in range(0, tile, chunk):
        at = slice(low, low + chunk)
        cosine = product((ih[at, :], ih8[at, :], il8[at, :]), texts_in, ((1,), (1,)))
        total = total + finish(at, cosine)
    loss[...] = total

    images_in = (ih[...], ih8[...], il8[...])
    sent = []
    for k, (out, (is_text, start, count)) in enumerate(zip(outs, kept)):
        base = start if is_text else tile + start
        step = min(count, 256)
        for low in range(0, count, step):
            at = slice(start + low, start + low + step)
            to = slice(base + low, base + low + step)
            if is_text:
                part = (wh[:, at], wh8[:, at], wl8[:, at])
                result[to, :] = product(part, images_in, ((0,), (0,)))
            else:
                part = (wh[at, :], wh8[at, :], wl8[at, :])
                result[to, :] = product(part, texts_in, ((1,), (0,)))
        copy = pltpu.make_async_copy(result.at[pl.ds(base, count)], out, sems.at[k])
        copy.start()
        sent.append(copy)
    for copy in sent:
        copy.wait()


def product(a, b, dims):
    dot = functools.partial(
        lax.dot_general, dimension_numbers=(dims, ((), ())), preferred_element_type=F32
    )
    small_part = dot(a[1], b[2]) + dot(a[2], b[1])
    return dot(a[0], b[0]) + small_part * (1.0 / (HIGH_UP * LOW_UP))


def back_body(*refs):
    a = refs[0:4]
    b = refs[4:8]
    text_sum, images, texts, loss, scal = refs[8:13]
    image_grad, text_grad, send = refs[13:]
    scale = scal[0]
    h = a[0].shape[0]
    squares = jnp.zeros((1, 1), F32)
    jobs = (
        (image_grad, images, 0, h, lambda: a[0][...] + a[1][...] + a[2][...] + a[3][...]),
        (image_grad, images, h, h, lambda: b[0][...] + b[1][...] + b[2][...] + b[3][...]),
        (text_grad, texts, 0, 2 * h, lambda: text_sum[...]),
    )
    for out, values, start, count, load in jobs:
        at = slice(start, start + count)
        g = scale * load()
        u, length = unit_rows(values[at, :])
        inner = jnp.sum(u * g, axis=1, keepdims=True)
        v = (g - u * inner) / length
        out[at, :] = v
        s = jnp.sum(v * v, axis=1, keepdims=True)
        squares = squares + jnp.sum(s, axis=0, keepdims=True)
    s = jnp.sum(loss[...], axis=1, keepdims=True)
    loss_sum = jnp.sum(s, axis=0, keepdims=True)
    lane = lax.broadcasted_iota(jnp.int32, send.shape, 2)
    send[...] = jnp.where(lane == 0, squares[None], jnp.where(lane == 1, loss_sum[None], 0.0))


def step_body(total, width, image_grad, text_grad, got, image_step, text_step, loss):
    sums = jnp.sum(got[...], axis=0)
    factor = lax.rsqrt(sums[:, 0:1] / (2.0 * total * width) + EPS)
    image_step[...] = image_grad[...] * factor
    text_step[...] = text_grad[...] * factor
    loss[0] = sums[0, 1] / (1.0 * total * total)


def local(images, texts, logit_scale, logit_bias):
    rows, d = images.shape
    h = rows // 2
    n = DEVICES * rows
    tile = 16 * rows
    y, core, z, x = (lax.axis_index(a).astype(jnp.int32) for a in NAMES)
    scal = jnp.concatenate([logit_scale, logit_bias])
    part = sds((h, d))
    first, second = call(unit_body, (part, part), (images,), limit=58)
    text_tile = lax.all_gather(texts, ("z", "core"), axis=0, tiled=False)
    text_tile = text_tile.reshape(SIZES["z"], 2, rows, d)
    pieces_a = gather_half(first, "x", "y")
    pieces_b = gather_half(second, "y", "x")
    pieces = pieces_a + pieces_b
    counts = tuple(p.shape[0] for p in pieces)

    places = [(0, s, f) for f, s in half_places()] + [(1, f, s) for f, s in half_places()]
    spot = jnp.stack([y, core, z, x])

    m = SIZES["z"]
    begin = [sum(counts[:k]) for k in range(len(counts))]
    order = (3, 4, 8, 9, 1, 2, 6, 7, 0, 5)
    kept = [(True, tile // 2, tile // 2), (True, 0, tile // 2)]
    kept += [(False, begin[k], counts[k]) for k in order]
    hbm = pl.BlockSpec(memory_space=pl.ANY)
    wide, wide8 = pltpu.VMEM((tile, d), BF16), pltpu.VMEM((tile, d), F8)
    square, square8 = pltpu.VMEM((tile, tile), BF16), pltpu.VMEM((tile, tile), F8)
    other, mine, *sums, loss = call(
        functools.partial(weight_body, tuple(places), min(512, tile), counts, kept),
        (*[sds((count, d)) for _, _, count in kept], sds((8, 128))),
        (*pieces, text_tile, scal, spot),
        specs=[hbm] * (len(pieces) + 1) + [SMEM, SMEM],
        out_specs=(*[hbm] * len(kept), VMEM),
        scratch=[
            *(wide, wide8, wide8, wide, wide8, wide8, square, square8, square8),
            pltpu.VMEM((tile, d), F32),
            pltpu.VMEM((m, 2, rows, d), F32),
            pltpu.VMEM((2 * tile, d), F32),
            pltpu.SemaphoreType.DMA((len(pieces) + m,)),
            pltpu.SemaphoreType.DMA((len(kept),)),
        ],
        limit=58,
        flops=14 * tile * tile * d,
        nbytes=tile * d * 16,
    )
    mine = mine + shift(other, "core", 1)
    mine, *sums[4:] = lax.optimization_barrier((mine, *sums[4:]))
    text_sum = lax.psum_scatter(mine, "z", scatter_dimension=0, tiled=True)
    parts = [sums[order.index(k)] for k in range(len(counts))]
    sums_a = reduce_half(parts[:5], "x", "y")
    sums_b = reduce_half(parts[5:], "y", "x")
    row = sds((rows, d))
    image_grad, text_grad, send = call(
        back_body,
        (row, row, sds((DEVICES, 1, 128))),
        (*sums_a, *sums_b, text_sum, images, texts, loss, scal),
        specs=[VMEM] * 12 + [SMEM],
    )
    got = lax.all_to_all(send, NAMES, 0, 0)
    image_step, text_step, loss = call(
        functools.partial(step_body, n, d),
        (row, row, sds((1,))),
        (image_grad, text_grad, got),
        out_specs=(VMEM, VMEM, SMEM),
    )
    return image_step, text_step, loss


def solution(mesh):
    fine = Mesh(mesh.devices.reshape(tuple(SIZES.values())), NAMES)
    image_spec = P(("y", "core", "z", "x"), None)
    text_spec = P(("z", "x", "y", "core"), None)
    return jax.shard_map(
        local,
        mesh=fine,
        in_specs=(image_spec, text_spec, P(), P()),
        out_specs=(image_spec, text_spec, P()),
        check_vma=False,
    )
```

```python
import functools

import jax
import jax.numpy as jnp
from jax import lax
from jax.experimental import pallas as pl
from jax.experimental.pallas import tpu as pltpu
from jax.sharding import Mesh, PartitionSpec as P

EPS = 1e-06
F32 = jnp.float32
BF16 = jnp.bfloat16
F8 = jnp.float8_e4m3fn
HIGH_UP = 2.0**8
LOW_UP = 2.0**17
SIZES = {"y": 4, "core": 2, "z": 8, "x": 4}
NAMES = tuple(SIZES)
DEVICES = 256
VMEM = pl.BlockSpec(memory_space=pltpu.VMEM)
SMEM = pl.BlockSpec(memory_space=pltpu.SMEM)


def call(body, out_shape, args, specs=None, out_specs=None, scratch=(), limit=8, flops=0, nbytes=0):
    return pl.pallas_call(
        body,
        out_shape=out_shape,
        in_specs=specs or [VMEM] * len(args),
        out_specs=out_specs or jax.tree.map(lambda _: VMEM, out_shape),
        scratch_shapes=list(scratch),
        compiler_params=pltpu.CompilerParams(vmem_limit_bytes=limit * 1024 * 1024),
        cost_estimate=pl.CostEstimate(flops=flops, bytes_accessed=nbytes, transcendentals=0),
    )(*args)


def sds(shape, dtype=F32):
    return jax.ShapeDtypeStruct(shape, dtype)


def shift(value, axis, step):
    n = SIZES[axis]
    return lax.ppermute(value, axis, [(i, (i + step) % n) for i in range(n)])


def unit_rows(v):
    length = jnp.sqrt(jnp.sum(v * v, axis=1, keepdims=True) + EPS)
    return v / length, length


def unit_body(image, first, second):
    h = first.shape[0]
    first[...] = unit_rows(image[:h, :])[0]
    second[...] = unit_rows(image[h:, :])[0]


def gather_half(value, first, second):
    h = value.shape[0]
    near = jnp.concatenate([value] + [shift(value, first, k) for k in (1, 2, 3)], axis=0)
    up = shift(near, second, 1)
    down = shift(near, second, -1)
    return [near, up, down, shift(up[: 2 * h], second, 1), shift(down[2 * h :], second, -1)]


def half_places():
    near = [0, -1, -2, -3]
    return [(f, s) for s in (0, -1, 1) for f in near] + [(f, 2) for f in near]


def reduce_half(parts, first, second):
    near, up, down, far_up, far_down = parts
    h = near.shape[0] // 4
    head = up[: 2 * h] + shift(far_up, second, -1)
    tail = down[2 * h :] + shift(far_down, second, 1)
    up = jnp.concatenate([head, up[2 * h :]], axis=0)
    down = jnp.concatenate([down[: 2 * h], tail], axis=0)
    near = near + shift(up, second, -1) + shift(down, second, 1)
    return [near[:h]] + [shift(near[k * h : (k + 1) * h], first, -k) for k in (1, 2, 3)]


def split(v):
    hi = v.astype(BF16)
    return hi, v - hi.astype(F32)


def small(hi, lo):
    return (hi.astype(F32) * HIGH_UP).astype(F8), (lo * LOW_UP).astype(F8)


def fold(v):
    r, c = v.shape
    v = v.reshape(r // 8, 8, c).sum(axis=0)
    out = v[:, :128]
    for k in range(1, c // 128):
        out = out + v[:, k * 128 : (k + 1) * 128]
    return out


def weight_body(places, chunk, counts, kept, *refs):
    n = len(counts)
    pieces = refs[:n]
    text, scal, spot = refs[n : n + 3]
    outs, loss = refs[n + 3 : n + 3 + len(kept)], refs[n + 3 + len(kept)]
    ih, ih8, il8, th, th8, tl8, wh, wh8, wl8, image_in, text_in, result, in_sems, sems = refs[
        n + 4 + len(kept) :
    ]
    m, rows = text.shape[0], text.shape[2]
    tile = ih.shape[0]
    h = rows // 2
    y, core, z, x = (spot[k] for k in range(4))

    image_copies, start = [], 0
    for k, count in enumerate(counts):
        at = pl.ds(start, count)
        image_copies.append(pltpu.make_async_copy(pieces[k], image_in.at[at], in_sems.at[k]))
        start += count
    text_copies = [
        pltpu.make_async_copy(text.at[k], text_in.at[k], in_sems.at[n + k]) for k in range(m)
    ]
    for copy in text_copies + image_copies:
        copy.start()

    def convert_images(low, high):
        start = 0
        for copy, count in zip(image_copies, counts):
            if low < start + count <= high:
                copy.wait()
            start += count
        at = slice(low, high)
        hi, lo = split(image_in[at, :])
        ih[at, :] = hi
        ih8[at, :], il8[at, :] = small(hi, lo)

    for k, copy in enumerate(text_copies):
        copy.wait()
        for c in (0, 1):
            at = slice((c * m + k) * rows, (c * m + k + 1) * rows)
            v = text_in[k, core if c == 0 else 1 - core]
            length = jnp.sqrt(jnp.sum(v * v, axis=1, keepdims=True) + EPS)
            hi, lo = split(v * (1.0 / length))
            th[at, :] = hi
            th8[at, :], tl8[at, :] = small(hi, lo)

    col = lax.broadcasted_iota(jnp.int32, (1, tile), 1)
    block = col // rows
    side = block // m
    text_core = jnp.where(side == 0, core, 1 - core)
    text_id = ((((block - side * m) * 4 + x) * 4 + y) * 2 + text_core) * rows + col % rows
    scale, bias = scal[0], scal[1]
    texts_in = (th[...], th8[...], tl8[...])

    def finish(at, cosine):
        logits = scale * cosine + bias
        parts = []
        for half, dy, dx in places[at.start // h : at.stop // h]:
            iy, ix = (y + dy) % 4, (x + dx) % 4
            first = (((iy * 2 + core) * 8 + z) * 4 + ix) * rows + half * h
            parts.append(first + lax.broadcasted_iota(jnp.int32, (h, 1), 0))
        image_id = jnp.concatenate(parts, axis=0)
        sign = jnp.where(image_id == text_id, -1.0, 1.0)
        v = sign * logits
        e = jnp.exp(-jnp.abs(v))
        u = 1.0 + e
        r = 1.0 / u
        w = sign * jnp.where(v >= 0.0, r, e * r)
        hi, lo = split(w)
        wh[at, :] = hi
        wh8[at, :], wl8[at, :] = small(hi, lo)
        return fold(jnp.maximum(v, 0.0) + jnp.log(u) + (e - (u - 1.0)) * r)

    total = jnp.zeros((8, 128), F32)
    convert_images(0, chunk)
    for low in range(0, tile, chunk):
        at = slice(low, low + chunk)
        cosine = product((ih[at, :], ih8[at, :], il8[at, :]), texts_in, ((1,), (1,)))
        if low + chunk < tile:
            convert_images(low + chunk, low + 2 * chunk)
        total = total + finish(at, cosine)
    loss[...] = total

    images_in = (ih[...], ih8[...], il8[...])
    step = min(256, tile // 2)
    sent = []

    def send(low, high):
        for k, (out, (start, count)) in enumerate(zip(outs, kept)):
            if low < start + count <= high:
                copy = pltpu.make_async_copy(result.at[pl.ds(start, count)], out, sems.at[k])
                copy.start()
                sent.append(copy)

    for low in list(range(tile // 2, tile, step)) + list(range(0, tile // 2, step)):
        at = slice(low, low + step)
        part = (wh[:, at], wh8[:, at], wl8[:, at])
        result[at, :] = product(part, images_in, ((0,), (0,)))
        send(low, low + step)
    for low in range(0, tile, step):
        at = slice(low, low + step)
        part = (wh[at, :], wh8[at, :], wl8[at, :])
        result[tile + low : tile + low + step, :] = product(part, texts_in, ((1,), (0,)))
        send(tile + low, tile + low + step)
    for copy in sent:
        copy.wait()


def product(a, b, dims):
    dot = functools.partial(
        lax.dot_general, dimension_numbers=(dims, ((), ())), preferred_element_type=F32
    )
    left = jnp.concatenate([a[1], a[2]], axis=dims[0][0])
    right = jnp.concatenate([b[2], b[1]], axis=dims[1][0])
    small_part = dot(left, right)
    return dot(a[0], b[0]) + small_part * (1.0 / (HIGH_UP * LOW_UP))


def back_body(*refs):
    a = refs[0:4]
    b = refs[4:8]
    text_sum, images, texts, loss, scal = refs[8:13]
    image_grad, text_grad, send = refs[13:]
    scale = scal[0]
    h = a[0].shape[0]
    squares = jnp.zeros((1, 1), F32)
    jobs = (
        (image_grad, images, 0, h, lambda: a[0][...] + a[1][...] + a[2][...] + a[3][...]),
        (image_grad, images, h, h, lambda: b[0][...] + b[1][...] + b[2][...] + b[3][...]),
        (text_grad, texts, 0, 2 * h, lambda: text_sum[...]),
    )
    for out, values, start, count, load in jobs:
        at = slice(start, start + count)
        g = scale * load()
        u, length = unit_rows(values[at, :])
        inner = jnp.sum(u * g, axis=1, keepdims=True)
        v = (g - u * inner) / length
        out[at, :] = v
        s = jnp.sum(v * v, axis=1, keepdims=True)
        squares = squares + jnp.sum(s, axis=0, keepdims=True)
    s = jnp.sum(loss[...], axis=1, keepdims=True)
    loss_sum = jnp.sum(s, axis=0, keepdims=True)
    lane = lax.broadcasted_iota(jnp.int32, send.shape, 2)
    send[...] = jnp.where(lane == 0, squares[None], jnp.where(lane == 1, loss_sum[None], 0.0))


def step_body(total, width, image_grad, text_grad, got, image_step, text_step, loss):
    sums = jnp.sum(got[...], axis=0)
    factor = lax.rsqrt(sums[:, 0:1] / (2.0 * total * width) + EPS)
    image_step[...] = image_grad[...] * factor
    text_step[...] = text_grad[...] * factor
    loss[0] = sums[0, 1] / (1.0 * total * total)


def local(images, texts, logit_scale, logit_bias):
    rows, d = images.shape
    h = rows // 2
    n = DEVICES * rows
    tile = 16 * rows
    y, core, z, x = (lax.axis_index(a).astype(jnp.int32) for a in NAMES)
    scal = jnp.concatenate([logit_scale, logit_bias])
    part = sds((h, d))
    first, second = call(unit_body, (part, part), (images,), limit=58)
    text_tile = lax.all_gather(texts, ("z", "core"), axis=0, tiled=False)
    text_tile = text_tile.reshape(SIZES["z"], 2, rows, d)
    pieces_a = gather_half(first, "x", "y")
    pieces_b = gather_half(second, "y", "x")
    pieces = pieces_a + pieces_b
    counts = tuple(p.shape[0] for p in pieces)

    places = [(0, s, f) for f, s in half_places()] + [(1, f, s) for f, s in half_places()]
    spot = jnp.stack([y, core, z, x])

    m = SIZES["z"]
    begin = [sum(counts[:k]) for k in range(len(counts))]
    order = (3, 4, 8, 9, 1, 2, 6, 7, 0, 5)
    kept = [(tile // 2, tile // 2), (0, tile // 2)]
    kept += [(tile + begin[k], counts[k]) for k in order]
    hbm = pl.BlockSpec(memory_space=pl.ANY)
    wide, wide8 = pltpu.VMEM((tile, d), BF16), pltpu.VMEM((tile, d), F8)
    square, square8 = pltpu.VMEM((tile, tile), BF16), pltpu.VMEM((tile, tile), F8)
    other, mine, *sums, loss = call(
        functools.partial(weight_body, tuple(places), min(256, tile), counts, kept),
        (*[sds((count, d)) for _, count in kept], sds((8, 128))),
        (*pieces, text_tile, scal, spot),
        specs=[hbm] * (len(pieces) + 1) + [SMEM, SMEM],
        out_specs=(*[hbm] * len(kept), VMEM),
        scratch=[
            *(wide, wide8, wide8, wide, wide8, wide8, square, square8, square8),
            pltpu.VMEM((tile, d), F32),
            pltpu.VMEM((m, 2, rows, d), F32),
            pltpu.VMEM((2 * tile, d), F32),
            pltpu.SemaphoreType.DMA((len(pieces) + m,)),
            pltpu.SemaphoreType.DMA((len(kept),)),
        ],
        limit=58,
        flops=14 * tile * tile * d,
        nbytes=tile * d * 16,
    )
    mine = mine + shift(other, "core", 1)
    mine, *sums[4:] = lax.optimization_barrier((mine, *sums[4:]))
    text_sum = lax.psum_scatter(mine, "z", scatter_dimension=0, tiled=True)
    parts = [sums[order.index(k)] for k in range(len(counts))]
    sums_a = reduce_half(parts[:5], "x", "y")
    sums_b = reduce_half(parts[5:], "y", "x")
    row = sds((rows, d))
    image_grad, text_grad, send = call(
        back_body,
        (row, row, sds((DEVICES, 1, 128))),
        (*sums_a, *sums_b, text_sum, images, texts, loss, scal),
        specs=[VMEM] * 12 + [SMEM],
    )
    got = lax.all_to_all(send, NAMES, 0, 0)
    image_step, text_step, loss = call(
        functools.partial(step_body, n, d),
        (row, row, sds((1,))),
        (image_grad, text_grad, got),
        out_specs=(VMEM, VMEM, SMEM),
    )
    return image_step, text_step, loss


def solution(mesh):
    fine = Mesh(mesh.devices.reshape(tuple(SIZES.values())), NAMES)
    image_spec = P(("y", "core", "z", "x"), None)
    text_spec = P(("z", "x", "y", "core"), None)
    return jax.shard_map(
        local,
        mesh=fine,
        in_specs=(image_spec, text_spec, P(), P()),
        out_specs=(image_spec, text_spec, P()),
        check_vma=False,
    )
```

```python
import functools

import jax
import jax.numpy as jnp
from jax import lax
from jax.experimental import pallas as pl
from jax.experimental.pallas import tpu as pltpu
from jax.sharding import Mesh, PartitionSpec as P

EPS = 1e-06
F32 = jnp.float32
BF16 = jnp.bfloat16
F8 = jnp.float8_e4m3fn
HIGH_UP = 2.0**8
LOW_UP = 2.0**17
SIZES = {"y": 4, "core": 2, "z": 8, "x": 4}
NAMES = tuple(SIZES)
DEVICES = 256
VMEM = pl.BlockSpec(memory_space=pltpu.VMEM)
SMEM = pl.BlockSpec(memory_space=pltpu.SMEM)


def call(body, out_shape, args, specs=None, out_specs=None, scratch=(), limit=8, flops=0, nbytes=0):
    return pl.pallas_call(
        body,
        out_shape=out_shape,
        in_specs=specs or [VMEM] * len(args),
        out_specs=out_specs or jax.tree.map(lambda _: VMEM, out_shape),
        scratch_shapes=list(scratch),
        compiler_params=pltpu.CompilerParams(vmem_limit_bytes=limit * 1024 * 1024),
        cost_estimate=pl.CostEstimate(flops=flops, bytes_accessed=nbytes, transcendentals=0),
    )(*args)


def sds(shape, dtype=F32):
    return jax.ShapeDtypeStruct(shape, dtype)


def shift(value, axis, step):
    n = SIZES[axis]
    return lax.ppermute(value, axis, [(i, (i + step) % n) for i in range(n)])


def unit_rows(v):
    length = jnp.sqrt(jnp.sum(v * v, axis=1, keepdims=True) + EPS)
    return v / length, length


def unit_body(image, first, second):
    h = first.shape[0]
    first[...] = unit_rows(image[:h, :])[0]
    second[...] = unit_rows(image[h:, :])[0]


def gather_half(value, first, second):
    h = value.shape[0]
    near = jnp.concatenate([value] + [shift(value, first, k) for k in (1, 2, 3)], axis=0)
    up = shift(near, second, 1)
    down = shift(near, second, -1)
    return [near, up, down, shift(up[: 2 * h], second, 1), shift(down[2 * h :], second, -1)]


def half_places():
    near = [0, -1, -2, -3]
    return [(f, s) for s in (0, -1, 1) for f in near] + [(f, 2) for f in near]


def reduce_half(parts, first, second):
    near, up, down, far_up, far_down = parts
    h = near.shape[0] // 4
    head = up[: 2 * h] + shift(far_up, second, -1)
    tail = down[2 * h :] + shift(far_down, second, 1)
    up = jnp.concatenate([head, up[2 * h :]], axis=0)
    down = jnp.concatenate([down[: 2 * h], tail], axis=0)
    near = near + shift(up, second, -1) + shift(down, second, 1)
    return [near[:h]] + [shift(near[k * h : (k + 1) * h], first, -k) for k in (1, 2, 3)]


def split(v):
    hi = v.astype(BF16)
    return hi, v - hi.astype(F32)


def small(hi, lo):
    return (hi.astype(F32) * HIGH_UP).astype(F8), (lo * LOW_UP).astype(F8)


def fold(v):
    r, c = v.shape
    v = v.reshape(r // 8, 8, c).sum(axis=0)
    out = v[:, :128]
    for k in range(1, c // 128):
        out = out + v[:, k * 128 : (k + 1) * 128]
    return out


def weight_body(places, chunk, counts, kept, *refs):
    n = len(counts)
    pieces = refs[:n]
    text, scal, spot = refs[n : n + 3]
    outs, loss = refs[n + 3 : n + 3 + len(kept)], refs[n + 3 + len(kept)]
    ih, ih8, il8, th, th8, tl8, wh, wh8, wl8, image_in, text_in, result, in_sems, sems = refs[
        n + 4 + len(kept) :
    ]
    m, rows = text.shape[0], text.shape[2]
    tile = ih.shape[0]
    h = rows // 2
    y, core, z, x = (spot[k] for k in range(4))

    image_copies, start = [], 0
    for k, count in enumerate(counts):
        at = pl.ds(start, count)
        image_copies.append(pltpu.make_async_copy(pieces[k], image_in.at[at], in_sems.at[k]))
        start += count
    text_copies = [
        pltpu.make_async_copy(text.at[k], text_in.at[k], in_sems.at[n + k]) for k in range(m)
    ]
    for copy in text_copies + image_copies:
        copy.start()

    def convert_images(low, high):
        start = 0
        for copy, count in zip(image_copies, counts):
            if low < start + count <= high:
                copy.wait()
            start += count
        at = slice(low, high)
        hi, lo = split(image_in[at, :])
        ih[at, :] = hi
        ih8[at, :], il8[at, :] = small(hi, lo)

    for k, copy in enumerate(text_copies):
        copy.wait()
        for c in (0, 1):
            at = slice((c * m + k) * rows, (c * m + k + 1) * rows)
            v = text_in[k, core if c == 0 else 1 - core]
            length = jnp.sqrt(jnp.sum(v * v, axis=1, keepdims=True) + EPS)
            hi, lo = split(v * (1.0 / length))
            th[at, :] = hi
            th8[at, :], tl8[at, :] = small(hi, lo)

    col = lax.broadcasted_iota(jnp.int32, (1, tile), 1)
    block = col // rows
    side = block // m
    text_core = jnp.where(side == 0, core, 1 - core)
    text_id = ((((block - side * m) * 4 + x) * 4 + y) * 2 + text_core) * rows + col % rows
    scale, bias = scal[0], scal[1]
    texts_in = (th[...], th8[...], tl8[...])

    def finish(at, cosine):
        logits = scale * cosine + bias
        parts = []
        for half, dy, dx in places[at.start // h : at.stop // h]:
            iy, ix = (y + dy) % 4, (x + dx) % 4
            first = (((iy * 2 + core) * 8 + z) * 4 + ix) * rows + half * h
            parts.append(first + lax.broadcasted_iota(jnp.int32, (h, 1), 0))
        image_id = jnp.concatenate(parts, axis=0)
        sign = jnp.where(image_id == text_id, -1.0, 1.0)
        v = sign * logits
        e = jnp.exp(-jnp.abs(v))
        u = 1.0 + e
        r = 1.0 / u
        w = sign * jnp.where(v >= 0.0, r, e * r)
        hi, lo = split(w)
        wh[at, :] = hi
        wh8[at, :], wl8[at, :] = small(hi, lo)
        return fold(jnp.maximum(v, 0.0) + jnp.log(u) + (e - (u - 1.0)) * r)

    total = jnp.zeros((8, 128), F32)
    convert_images(0, chunk)
    for low in range(0, tile, chunk):
        at = slice(low, low + chunk)
        cosine = product((ih[at, :], ih8[at, :], il8[at, :]), texts_in, ((1,), (1,)))
        if low + chunk < tile:
            convert_images(low + chunk, low + 2 * chunk)
        total = total + finish(at, cosine)
    loss[...] = total

    images_in = (ih[...], ih8[...], il8[...])
    step = min(256, tile // 2)
    sent = []

    def send(low, high):
        for k, (out, (start, count)) in enumerate(zip(outs, kept)):
            if low < start + count <= high:
                copy = pltpu.make_async_copy(result.at[pl.ds(start, count)], out, sems.at[k])
                copy.start()
                sent.append(copy)

    for low in list(range(tile // 2, tile, step)) + list(range(0, tile // 2, step)):
        at = slice(low, low + step)
        part = (wh[:, at], wh8[:, at], wl8[:, at])
        result[at, :] = product(part, images_in, ((0,), (0,)))
        send(low, low + step)
    for low in range(0, tile, step):
        at = slice(low, low + step)
        part = (wh[at, :], wh8[at, :], wl8[at, :])
        result[tile + low : tile + low + step, :] = product(part, texts_in, ((1,), (0,)))
        send(tile + low, tile + low + step)
    for copy in sent:
        copy.wait()


def product(a, b, dims):
    dot = functools.partial(
        lax.dot_general, dimension_numbers=(dims, ((), ())), preferred_element_type=F32
    )
    left = jnp.concatenate([a[1], a[2]], axis=dims[0][0])
    right = jnp.concatenate([b[2], b[1]], axis=dims[1][0])
    small_part = dot(left, right)
    return dot(a[0], b[0]) + small_part * (1.0 / (HIGH_UP * LOW_UP))


def back_body(*refs):
    a = refs[0:4]
    b = refs[4:8]
    text_sum, images, texts, loss, scal = refs[8:13]
    image_grad, text_grad, send = refs[13:]
    scale = scal[0]
    h = a[0].shape[0]
    squares = jnp.zeros((1, 1), F32)
    jobs = (
        (image_grad, images, 0, h, lambda: a[0][...] + a[1][...] + a[2][...] + a[3][...]),
        (image_grad, images, h, h, lambda: b[0][...] + b[1][...] + b[2][...] + b[3][...]),
        (text_grad, texts, 0, 2 * h, lambda: text_sum[...]),
    )
    for out, values, start, count, load in jobs:
        at = slice(start, start + count)
        g = scale * load()
        u, length = unit_rows(values[at, :])
        inner = jnp.sum(u * g, axis=1, keepdims=True)
        v = (g - u * inner) / length
        out[at, :] = v
        s = jnp.sum(v * v, axis=1, keepdims=True)
        squares = squares + jnp.sum(s, axis=0, keepdims=True)
    s = jnp.sum(loss[...], axis=1, keepdims=True)
    loss_sum = jnp.sum(s, axis=0, keepdims=True)
    lane = lax.broadcasted_iota(jnp.int32, send.shape, 2)
    send[...] = jnp.where(lane == 0, squares[None], jnp.where(lane == 1, loss_sum[None], 0.0))


def step_body(total, width, image_grad, text_grad, got, image_step, text_step, loss):
    sums = jnp.sum(got[...], axis=0)
    factor = lax.rsqrt(sums[:, 0:1] / (2.0 * total * width) + EPS)
    image_step[...] = image_grad[...] * factor
    text_step[...] = text_grad[...] * factor
    loss[0] = sums[0, 1] / (1.0 * total * total)


def local(images, texts, logit_scale, logit_bias):
    rows, d = images.shape
    h = rows // 2
    n = DEVICES * rows
    tile = 16 * rows
    y, core, z, x = (lax.axis_index(a).astype(jnp.int32) for a in NAMES)
    scal = jnp.concatenate([logit_scale, logit_bias])
    part = sds((h, d))
    first, second = call(unit_body, (part, part), (images,), limit=58)
    text_tile = lax.all_gather(texts, ("z", "core"), axis=0, tiled=False)
    text_tile = text_tile.reshape(SIZES["z"], 2, rows, d)
    pieces_a = gather_half(first, "x", "y")
    pieces_b = gather_half(second, "y", "x")
    pieces = pieces_a + pieces_b
    counts = tuple(p.shape[0] for p in pieces)

    places = [(0, s, f) for f, s in half_places()] + [(1, f, s) for f, s in half_places()]
    spot = jnp.stack([y, core, z, x])

    m = SIZES["z"]
    begin = [sum(counts[:k]) for k in range(len(counts))]
    order = (3, 4, 8, 9, 1, 2, 6, 7, 0, 5)
    kept = [(tile // 2, tile // 2), (0, tile // 2)]
    kept += [(tile + begin[k], counts[k]) for k in order]
    hbm = pl.BlockSpec(memory_space=pl.ANY)
    wide, wide8 = pltpu.VMEM((tile, d), BF16), pltpu.VMEM((tile, d), F8)
    square, square8 = pltpu.VMEM((tile, tile), BF16), pltpu.VMEM((tile, tile), F8)
    other, mine, *sums, loss = call(
        functools.partial(weight_body, tuple(places), min(256, tile), counts, kept),
        (*[sds((count, d)) for _, count in kept], sds((8, 128))),
        (*pieces, text_tile, scal, spot),
        specs=[hbm] * (len(pieces) + 1) + [SMEM, SMEM],
        out_specs=(*[hbm] * len(kept), VMEM),
        scratch=[
            *(wide, wide8, wide8, wide, wide8, wide8, square, square8, square8),
            pltpu.VMEM((tile, d), F32),
            pltpu.VMEM((m, 2, rows, d), F32),
            pltpu.VMEM((2 * tile, d), F32),
            pltpu.SemaphoreType.DMA((len(pieces) + m,)),
            pltpu.SemaphoreType.DMA((len(kept),)),
        ],
        limit=58,
        flops=14 * tile * tile * d,
        nbytes=tile * d * 16,
    )
    mine = mine + shift(other, "core", 1)
    mine, *sums[3:] = lax.optimization_barrier((mine, *sums[3:]))
    text_sum = lax.psum_scatter(mine, "z", scatter_dimension=0, tiled=True)
    parts = [sums[order.index(k)] for k in range(len(counts))]
    sums_a = reduce_half(parts[:5], "x", "y")
    sums_b = reduce_half(parts[5:], "y", "x")
    row = sds((rows, d))
    image_grad, text_grad, send = call(
        back_body,
        (row, row, sds((DEVICES, 1, 128))),
        (*sums_a, *sums_b, text_sum, images, texts, loss, scal),
        specs=[VMEM] * 12 + [SMEM],
    )
    got = lax.all_to_all(send, NAMES, 0, 0)
    image_step, text_step, loss = call(
        functools.partial(step_body, n, d),
        (row, row, sds((1,))),
        (image_grad, text_grad, got),
        out_specs=(VMEM, VMEM, SMEM),
    )
    return image_step, text_step, loss


def solution(mesh):
    fine = Mesh(mesh.devices.reshape(tuple(SIZES.values())), NAMES)
    image_spec = P(("y", "core", "z", "x"), None)
    text_spec = P(("z", "x", "y", "core"), None)
    return jax.shard_map(
        local,
        mesh=fine,
        in_specs=(image_spec, text_spec, P(), P()),
        out_specs=(image_spec, text_spec, P()),
        check_vma=False,
    )
```
